32 devices in a mesh: dp: 8 (over z, x), tensor: 4 (over y, core).
Axes of the slice: x: 2, y: 2, z: 4, core: 2. Of those that a mesh axis runs over, the one named last changes fastest.
Arguments:
- activations: bfloat16 [1024, 14336], P('dp', 'tensor'), may hold values from -6 to 6
- in_basis: bfloat16 [14336, 8192], P('tensor', 'dp'), may hold values from -0.046875 to 0.046875
- out_grads: bfloat16 [1024, 4096], P('dp', 'tensor'), may hold values from -6 to 6
- out_basis: bfloat16 [4096, 4096], P(None, 'tensor'), may hold values from -0.09375 to 0.09375
- doc_lengths: int32 [8], replicated, may hold values from 1 to 256, 1024 in all
Outputs:
- corrections: float32 [8192, 4096], P('dp', 'tensor')
The draws below stay inside these ranges and needn't reach their ends.
Inputs may be any that keep to these rules, and one draw needn't show every extreme that they name: `doc_lengths`: 8 lengths that sum to 1024; the longest is exactly 256.
All inputs are finite; a program needn't handle non-finite values.
Results may differ from the reference program's by a relative error of at most 0.0018.
Values may be sent and summed in bfloat16 or wider, within the bound.
No kernel may reach another device: no remote copies, remote signals or barrier semaphores. Data moves between devices by JAX's collectives and lax.ppermute only.
A program may use at most 64 MiB of HBM per device.

```python
import math
import jax
import jax.numpy as jnp
import numpy as np
from jax import lax

D = 4096
FF = 14336
JW = 8192
MAXLEN = 256
TOKENS = 1024
DOCS = 8


def level_of(rng, dims, pieces, smallest, largest):
    level = 1.0
    for axis_at, shards_of in pieces:
        heights = jax.random.uniform(jax.random.fold_in(jax.random.fold_in(rng, 6), axis_at), (shards_of,), jnp.float32, smallest / len(pieces), largest / len(pieces))
        level = level * jnp.repeat(jnp.exp(heights), dims[axis_at] // shards_of).reshape((-1,) + (1,) * (len(dims) - 1 - axis_at))
    return level


def split_up(count, total, most, skew):
    portions = [(1 << 20) // math.isqrt(grade ** skew) + 1 for grade in range(2, count + 1)]
    spare, holding = total - most - (count - 1), [1] * (count - 1)
    while spare > 0:
        movable = [i for i in range(count - 1) if holding[i] < most]
        pool, budget = sum([portions[i] for i in movable]), spare
        for i in movable:
            more = min(most - holding[i], max(1, budget * portions[i] // pool), spare)
            holding[i] = holding[i] + more
            spare = spare - more
    return np.array([most] + holding)


def uneven(rng, number_of, total, most, skew):
    if number_of == 2:
        one = jax.random.randint(rng, (), max(1, total - most), min(most, total - 1) + 1)
        return jnp.stack([one, total - one])
    tallies = jnp.asarray(split_up(number_of, total, most, skew), jnp.int32)
    couples = (number_of - 1) // 2
    giver, receiver = tallies[1:1 + 2 * couples:2], tallies[2:2 + 2 * couples:2]
    slack = jnp.minimum(giver - 1, most - receiver)
    shifted = jax.random.randint(jax.random.fold_in(rng, 1), (couples,), 0, 1 << 20) % (slack + 1)
    tallies = tallies.at[1:1 + 2 * couples:2].set(giver - shifted).at[2:2 + 2 * couples:2].set(receiver + shifted)
    return tallies[jax.random.permutation(jax.random.fold_in(rng, 2), number_of)]


def gaussian(own_key, shape, width, limit, split=(), kind=jnp.bfloat16):
    drawn = jax.random.normal(own_key, shape, jnp.float32) * width
    if len(split) > 0:
        drawn = level_of(own_key, shape, split, -0.22, 0.18) * drawn
    return jnp.clip(drawn, min=-limit, max=limit).astype(kind)


def setup_inputs(seed: int = 0) -> dict:
    streams_of = jax.random.split(jax.random.key(seed), 6)
    activations = gaussian(streams_of[0], (TOKENS, FF), 1.0, 6.0, ((0, 8), (1, 4)))
    in_basis = gaussian(streams_of[1], (FF, JW), FF ** -0.5, 0.046875, ((0, 4), (1, 8)))
    out_grads = gaussian(streams_of[2], (TOKENS, D), 1.0, 6.0, ((0, 8), (1, 4)))
    out_basis = gaussian(streams_of[3], (D, D), D ** -0.5, 0.09375, ((1, 4),))
    doc_lengths = uneven(streams_of[4], DOCS, TOKENS, MAXLEN, 2).astype(jnp.int32)
    return {"activations": activations, "in_basis": in_basis, "out_grads": out_grads, "out_basis": out_basis, "doc_lengths": doc_lengths}


def document_squares(rotated, grad_rows, doc_lengths, window):
    starts = (jnp.cumsum(doc_lengths) - doc_lengths).astype(jnp.int32)
    pad_in = jnp.concatenate([rotated, jnp.zeros((window, rotated.shape[1]), rotated.dtype)], 0)
    pad_out = jnp.concatenate([grad_rows, jnp.zeros((window, grad_rows.shape[1]), grad_rows.dtype)], 0)
    offsets = jnp.arange(window, dtype=jnp.int32)

    def advance(running, inputs_pair):
        begin, length = inputs_pair
        left_rows = lax.dynamic_slice_in_dim(pad_in, begin, window, 0).astype(jnp.float32)
        right_rows = lax.dynamic_slice_in_dim(pad_out, begin, window, 0).astype(jnp.float32)
        row_mask = (offsets < length).astype(jnp.float32)
        left_rows = left_rows * row_mask[:, None]
        blocks = jnp.dot(left_rows.T, right_rows, preferred_element_type=jnp.float32)
        return running + blocks * blocks, None

    initial = jnp.zeros((rotated.shape[1], grad_rows.shape[1]), jnp.float32)
    summed, unused = lax.scan(advance, initial, (starts, doc_lengths.astype(jnp.int32)))
    return summed


def reference(activations, in_basis, out_grads, out_basis, doc_lengths):
    rotated = jnp.dot(activations, in_basis, preferred_element_type=jnp.float32).astype(jnp.bfloat16)
    grad_rows = jnp.dot(out_grads, out_basis, preferred_element_type=jnp.float32).astype(jnp.bfloat16)
    summed = document_squares(rotated, grad_rows, doc_lengths, MAXLEN)
    return summed / jnp.float32(TOKENS)
```

```python
import functools

import jax
import jax.numpy as jnp
import numpy as np
from jax import lax
from jax.experimental import pallas as pl
from jax.experimental.pallas import tpu as pltpu
from jax.sharding import PartitionSpec as P

MAXLEN = 256
ROWS = 16
SUBS = 1


def ring_order(count):
    return list(range(0, count, 2)) + list(range(1, count, 2))[::-1]


def document_kernel(window, starts_ref, lengths_ref, rotated_ref, grads_ref, out_ref):
    tokens = rotated_ref.shape[0]
    documents = starts_ref.shape[0]

    def masked(base, size, first, last):
        row = base + lax.broadcasted_iota(jnp.int32, (size, 1), 0)
        keep = jnp.logical_and(row >= first, row < last)
        left = rotated_ref[pl.ds(base, size), :]
        left = jnp.where(keep, left, jnp.zeros_like(left))
        right = grads_ref[pl.ds(base, size), :]
        return lax.dot_general(
            left, right, (((0,), (0,)), ((), ())), preferred_element_type=jnp.float32
        )

    out_ref[...] = jnp.zeros_like(out_ref)

    def one(s, carry):
        first = starts_ref[s]
        last = first + lengths_ref[s]
        base = jnp.minimum((first // ROWS) * ROWS, tokens - window)
        base = pl.multiple_of(base, ROWS)
        fits = last <= base + window

        @pl.when(fits)
        def _():
            block = masked(base, window, first, last)
            out_ref[...] += block * block

        @pl.when(jnp.logical_not(fits))
        def _():
            block = masked(base, window, first, last)
            rest = pl.multiple_of(base + window, ROWS)
            block = block + masked(rest, ROWS, first, last)
            out_ref[...] += block * block

        return carry

    lax.fori_loop(0, documents, one, 0)
    out_ref[...] = out_ref[...] * jnp.float32(1.0 / tokens)


def document_squares(rotated, grad_rows, doc_lengths):
    tokens, width = rotated.shape
    columns = grad_rows.shape[1]
    starts = (jnp.cumsum(doc_lengths) - doc_lengths).astype(jnp.int32)
    tile = min(256, width)
    return pl.pallas_call(
        functools.partial(document_kernel, MAXLEN),
        out_shape=jax.ShapeDtypeStruct((width, columns), jnp.float32),
        grid_spec=pltpu.PrefetchScalarGridSpec(
            num_scalar_prefetch=2,
            grid=(width // tile,),
            in_specs=[
                pl.BlockSpec((tokens, tile), lambda j, *_: (0, j)),
                pl.BlockSpec((tokens, columns), lambda j, *_: (0, 0)),
            ],
            out_specs=pl.BlockSpec((tile, columns), lambda j, *_: (j, 0)),
        ),
        compiler_params=pltpu.CompilerParams(vmem_limit_bytes=32 * 1024 * 1024),
        cost_estimate=pl.CostEstimate(
            flops=2 * MAXLEN * doc_lengths.shape[0] * width * columns,
            bytes_accessed=2 * tokens * (width + columns) + 4 * width * columns,
            transcendentals=0,
        ),
    )(starts, doc_lengths.astype(jnp.int32), rotated, grad_rows)


def solution(mesh):
    n_dp, n_tensor = mesh.shape["dp"], mesh.shape["tensor"]
    order = ring_order(n_dp)
    place = np.argsort(np.array(order))
    forward = [(order[i], order[(i + 1) % n_dp]) for i in range(n_dp)]
    backward = [(d, s) for s, d in forward]
    swaps = {d: [(t, t ^ d) for t in range(n_tensor)] for d in range(1, n_tensor)}

    def sum_over_tensor(partial_value):
        me = lax.axis_index("tensor")
        rows = partial_value.shape[0] // n_tensor

        def share(t):
            return lax.dynamic_slice_in_dim(partial_value, t * rows, rows, 0)

        got = [lax.ppermute(share(me ^ d), "tensor", swaps[d]) for d in range(1, n_tensor)]
        total = share(me)
        for piece in got:
            total = total + piece
        total = total.astype(jnp.bfloat16)
        blocks = [(me, total)]
        for d in range(1, n_tensor):
            blocks.append((me ^ d, lax.ppermute(total, "tensor", swaps[d])))
        whole = jnp.zeros(partial_value.shape, jnp.bfloat16)
        for t, block in blocks:
            whole = lax.dynamic_update_slice_in_dim(whole, block, t * rows, 0)
        return whole

    def local(activations, in_basis, out_grads, out_basis, doc_lengths):
        mine = lax.axis_index("dp")
        spot = jnp.asarray(place, jnp.int32)[mine]
        shard = activations.shape[0]
        tokens = shard * n_dp
        half = shard // 2
        sub = half // SUBS

        def origin(step):
            return jnp.asarray(order, jnp.int32)[(spot + step) % n_dp]

        def start_of(source, way, k):
            return source * shard + way * half + k * sub

        def ring(block, subs):
            rows = half // subs
            moving = [
                (way, k, block[way * half + k * rows : way * half + (k + 1) * rows])
                for k in range(subs)
                for way in (0, 1)
            ]
            hops = [[(mine * shard, block)]]
            for h in range(1, n_dp):
                moving = [
                    (way, k, lax.ppermute(v, "dp", (forward, backward)[way]))
                    for way, k, v in moving
                ]
                hops.append(
                    [
                        (origin(-h if way == 0 else h) * shard + way * half + k * rows, v)
                        for way, k, v in moving
                    ]
                )
            return hops

        features = lax.all_gather(out_grads, "tensor", axis=1, tiled=True)
        own_grads = jnp.dot(features, out_basis, preferred_element_type=jnp.float32)
        own_grads = own_grads.astype(jnp.bfloat16)

        act_hops = ring(activations, SUBS)
        rotated = jnp.zeros((tokens, in_basis.shape[1]), jnp.bfloat16)
        groups = [[0, 1]] + [[h, h + 1] for h in range(2, n_dp - 2, 2)] + [[n_dp - 2], [n_dp - 1]]
        for group in groups:
            pieces = [piece for h in group for piece in act_hops[h]]
            stacked = jnp.concatenate([v for _, v in pieces], 0)
            partial_value = jnp.dot(stacked, in_basis, preferred_element_type=jnp.float32)
            done = sum_over_tensor(partial_value)
            at = 0
            for offset, v in pieces:
                rotated = lax.dynamic_update_slice_in_dim(
                    rotated, done[at : at + v.shape[0]], offset, 0
                )
                at += v.shape[0]

        grad_rows = jnp.zeros((tokens, own_grads.shape[1]), jnp.bfloat16)
        for hop in ring(own_grads, 1):
            for offset, v in hop:
                grad_rows = lax.dynamic_update_slice_in_dim(grad_rows, v, offset, 0)

        return document_squares(rotated, grad_rows, doc_lengths)

    placed = (P("dp", "tensor"), P("tensor", "dp"), P("dp", "tensor"), P(None, "tensor"), P())
    return jax.shard_map(
        local, mesh=mesh, in_specs=placed, out_specs=P("dp", "tensor"), check_vma=False
    )
```

```python
import functools

import jax
import jax.numpy as jnp
from jax import lax
from jax.experimental import pallas as pl
from jax.experimental.pallas import tpu as pltpu
from jax.sharding import PartitionSpec as P

MAXLEN = 256
LAG = 3
WAIT_SHARES = 2
WAIT_SUM = 1


def ring_order(count):
    return list(range(0, count, 2)) + list(range(1, count, 2))[::-1]


def document_kernel(window, lengths_ref, rotated_ref, grads_ref, out_ref, turned_ref):
    tokens = rotated_ref.shape[0]
    documents = lengths_ref.shape[0]

    for at in range(0, tokens, window):
        turned_ref[:, at : at + window] = rotated_ref[at : at + window, :].T

    def product(block, first, last):
        base = pl.multiple_of(block * window, window)
        row = base + lax.broadcasted_iota(jnp.int32, (window, 1), 0)
        keep = jnp.logical_and(row >= first, row < last)
        right = grads_ref[pl.ds(base, window), :]
        right = jnp.where(keep, right, jnp.zeros_like(right))
        left = turned_ref[:, pl.ds(base, window)]
        return jnp.dot(left, right, preferred_element_type=jnp.float32)

    def add(s, value):
        value = value * value
        if s > 0:
            value = out_ref[...] + value
        if s == documents - 1:
            value = value * jnp.float32(1.0 / tokens)
        out_ref[...] = value

    first = jnp.int32(0)
    for s in range(documents):
        last = first + lengths_ref[s]
        low, high = first // window, (last - 1) // window

        @pl.when(low == high)
        def _(s=s, low=low, first=first, last=last):
            add(s, product(low, first, last))

        @pl.when(low != high)
        def _(s=s, low=low, high=high, first=first, last=last):
            add(s, product(low, first, last) + product(high, first, last))

        first = last


def document_squares(rotated, grad_rows, doc_lengths):
    tokens, width = rotated.shape
    columns = grad_rows.shape[1]
    return pl.pallas_call(
        functools.partial(document_kernel, MAXLEN),
        out_shape=jax.ShapeDtypeStruct((width, columns), jnp.float32),
        in_specs=[
            pl.BlockSpec(memory_space=pltpu.SMEM),
            pl.BlockSpec(memory_space=pltpu.VMEM),
            pl.BlockSpec(memory_space=pltpu.VMEM),
        ],
        out_specs=pl.BlockSpec(memory_space=pltpu.VMEM),
        scratch_shapes=[pltpu.VMEM((width, tokens), jnp.bfloat16)],
        compiler_params=pltpu.CompilerParams(vmem_limit_bytes=40 * 1024 * 1024),
        cost_estimate=pl.CostEstimate(
            flops=2 * MAXLEN * doc_lengths.shape[0] * width * columns,
            bytes_accessed=2 * tokens * (width + columns) + 4 * width * columns,
            transcendentals=0,
        ),
    )(doc_lengths.astype(jnp.int32), rotated, grad_rows)


def rotate_kernel(hidden, *refs):
    *pieces, basis_ref, out_ref = refs
    rows = [ref[:, :hidden] for ref in pieces]
    stacked = jnp.concatenate(rows, 0) if len(rows) > 1 else rows[0]
    out_ref[...] = jnp.dot(stacked, basis_ref[...], preferred_element_type=jnp.float32)


def rotate(pieces, basis):
    hidden, width = basis.shape
    rows = sum(v.shape[0] for v in pieces)
    return pl.pallas_call(
        functools.partial(rotate_kernel, hidden),
        out_shape=jax.ShapeDtypeStruct((rows, width), jnp.float32),
        in_specs=[pl.BlockSpec(memory_space=pltpu.VMEM)] * (len(pieces) + 1),
        out_specs=pl.BlockSpec(memory_space=pltpu.VMEM),
        compiler_params=pltpu.CompilerParams(vmem_limit_bytes=16 * 1024 * 1024),
        cost_estimate=pl.CostEstimate(flops=0, bytes_accessed=0, transcendentals=0),
    )(*pieces, basis)


def solution(mesh):
    n_dp, n_tensor = mesh.shape["dp"], mesh.shape["tensor"]
    order = ring_order(n_dp)
    forward = [(order[i], order[(i + 1) % n_dp]) for i in range(n_dp)]
    backward = [(d, s) for s, d in forward]
    swaps = {d: [(t, t ^ d) for t in range(n_tensor)] for d in range(1, n_tensor)}

    def local(activations, in_basis, out_grads, out_basis, doc_lengths):
        in_basis = pltpu.with_memory_space_constraint(in_basis, pltpu.VMEM)
        mine = lax.axis_index("dp")
        me = lax.axis_index("tensor")
        spot = jnp.where(mine % 2 == 0, mine // 2, n_dp - 1 - mine // 2)
        shard = activations.shape[0]
        half = shard // 2
        tokens = shard * n_dp
        columns = out_basis.shape[1]

        def offset_of(hop, way):
            step = -hop if way == 0 else hop
            at = (spot + step) % n_dp
            source = jnp.where(2 * at < n_dp, 2 * at, 2 * (n_dp - 1 - at) + 1)
            return source * shard + way * half

        def pieces_of(block):
            return [block[:half], block[half:]]

        def pass_on(pieces):
            return [lax.ppermute(v, "dp", p) for v, p in zip(pieces, (forward, backward))]

        def share(values, t):
            rows = shard // n_tensor
            own = [lax.dynamic_slice_in_dim(v, t * rows, rows, 0) for v in values]
            return jnp.concatenate(own, 0)

        def send_shares(values):
            got = [
                lax.ppermute(share(values, me ^ d), "tensor", swaps[d])
                for d in range(1, n_tensor)
            ]
            return [share(values, me)] + got

        def send_sum(parts):
            total = functools.reduce(jnp.add, parts).astype(jnp.bfloat16)
            return [total] + [lax.ppermute(total, "tensor", swaps[d]) for d in range(1, n_tensor)]

        def by_peer(blocks, axis):
            size = blocks[0].shape[axis]
            shape = list(blocks[0].shape)
            shape[axis] *= n_tensor
            value = jnp.zeros(shape, blocks[0].dtype)
            for d, block in enumerate(blocks):
                value = lax.dynamic_update_slice_in_dim(value, block, (me ^ d) * size, axis)
            return value

        hops = n_dp - 1 + LAG
        groups = [list(range(0, 3))] + [[h, h + 1] for h in range(3, n_dp - 2, 2)]
        groups += [list(range(groups[-1][-1] + 1, n_dp))]

        act = {0: pieces_of(activations)}
        grads, partials, sums = {}, {}, {}
        flight = pass_on(act[0])
        gathered = [out_grads]
        gathered += [lax.ppermute(out_grads, "tensor", swaps[d]) for d in range(1, n_tensor)]
        partials[0] = rotate(act[0], in_basis)
        due = {1: [("features", 0, gathered)], 2: []}

        def later(hop, kind, i, value):
            due.setdefault(hop, []).append((kind, i, value))

        for hop in range(1, hops + 1):
            ready = due.pop(hop, [])
            bundle = (flight, [value for _, _, value in ready])
            arrived, values = lax.optimization_barrier(bundle)
            for (kind, i, _), value in zip(ready, values):
                if kind == "features":
                    product = jnp.dot(
                        by_peer(value, 1), out_basis, preferred_element_type=jnp.float32
                    )
                    later(hop + 1, "own", 0, product.astype(jnp.bfloat16))
                elif kind == "own":
                    grads[0] = pieces_of(value)
                elif kind == "shares":
                    later(hop + WAIT_SUM, "sums", i, send_sum(value))
                elif kind == "sums":
                    sums[i] = value
                else:
                    partials[i] = value
            if hop < n_dp:
                act[hop] = arrived
            if hop > LAG:
                grads[hop - LAG] = [v[:, -columns:] for v in arrived]
            moving = arrived
            if hop == LAG:
                moving = [jnp.concatenate([v, g], 1) for v, g in zip(arrived, grads[0])]
            if hop == n_dp - 1:
                moving = grads[hop - LAG]
            if hop < hops:
                flight = pass_on(moving)
            if hop < n_dp:
                partials[hop] = rotate(act[hop], in_basis)
            for i, group in enumerate(groups):
                if group[-1] == hop:
                    parts = send_shares([partials[h] for h in group])
                    if hop < n_dp - 1:
                        later(hop + WAIT_SHARES, "shares", i, parts)
                    else:
                        sums[i] = send_sum(parts)

        for _, items in sorted(due.items()):
            for kind, i, value in items:
                sums[i] = send_sum(value) if kind == "shares" else value

        rotated = jnp.zeros((tokens, in_basis.shape[1]), jnp.bfloat16)
        rows = shard // n_tensor
        for i, group in enumerate(groups):
            for j, h in enumerate(group):
                value = by_peer([v[j * rows : (j + 1) * rows] for v in sums[i]], 0)
                for way, piece in enumerate(pieces_of(value)):
                    rotated = lax.dynamic_update_slice_in_dim(
                        rotated, piece, offset_of(h, way), 0
                    )
        grad_rows = jnp.zeros((tokens, columns), jnp.bfloat16)
        for h, pieces in grads.items():
            for way, piece in enumerate(pieces):
                grad_rows = lax.dynamic_update_slice_in_dim(
                    grad_rows, piece, offset_of(h, way), 0
                )
        return document_squares(rotated, grad_rows, doc_lengths)

    placed = (P("dp", "tensor"), P("tensor", "dp"), P("dp", "tensor"), P(None, "tensor"), P())
    return jax.shard_map(
        local, mesh=mesh, in_specs=placed, out_specs=P("dp", "tensor"), check_vma=False
    )
```

```python
import functools

import jax
import jax.numpy as jnp
from jax import lax
from jax.experimental import pallas as pl
from jax.experimental.pallas import tpu as pltpu
from jax.sharding import PartitionSpec as P

MAXLEN = 256
LAG = 3
TILE = 16
SMALL_VMEM = 8 * 1024 * 1024
DOCUMENT_VMEM = 20 * 1024 * 1024
FREE = pl.CostEstimate(flops=0, bytes_accessed=0, transcendentals=0)
SMEM = pl.BlockSpec(memory_space=pltpu.SMEM)
VMEM = pl.BlockSpec(memory_space=pltpu.VMEM)
ANY = pl.BlockSpec(memory_space=pl.ANY)


def ring_order(count):
    return list(range(0, count, 2)) + list(range(1, count, 2))[::-1]


def call(kernel, shapes, in_specs, *operands, scratch=()):
    return pl.pallas_call(
        kernel,
        out_shape=[jax.ShapeDtypeStruct(*shape) for shape in shapes],
        in_specs=in_specs,
        out_specs=[VMEM] * len(shapes),
        scratch_shapes=list(scratch),
        compiler_params=pltpu.CompilerParams(vmem_limit_bytes=SMALL_VMEM),
        cost_estimate=FREE,
    )(*operands)


def product_of(piece_refs, basis_ref):
    hidden = basis_ref.shape[0]
    pieces = [ref[:, :hidden] for ref in piece_refs]
    return jnp.dot(
        jnp.concatenate(pieces, 0), basis_ref[...], preferred_element_type=jnp.float32
    )


def rotate_pair_kernel(me_ref, *refs):
    *piece_refs, basis_ref, kept_ref, sent_ref = refs
    product = product_of(piece_refs, basis_ref)
    rows = product.shape[0] // 2
    low = me_ref[0] % 2 == 0
    kept_ref[...] = jnp.where(low, product[:rows], product[rows:])
    sent_ref[...] = jnp.where(low, product[rows:], product[:rows])


def rotate_pair(me, pieces, basis):
    rows = sum(v.shape[0] for v in pieces) // 2
    shape = ((rows, basis.shape[1]), jnp.float32)
    specs = [SMEM] + [VMEM] * (len(pieces) + 1)
    return call(rotate_pair_kernel, [shape] * 2, specs, me, *pieces, basis)


def rotate_shares_kernel(count, me_ref, *refs):
    piece_refs, (basis_ref, *share_refs, product_ref) = refs[:-count - 2], refs[-count - 2 :]
    product_ref[...] = product_of(piece_refs, basis_ref)
    rows = share_refs[0].shape[0]
    for d, share_ref in enumerate(share_refs):
        at = pl.multiple_of((me_ref[0] ^ d) * rows, rows)
        share_ref[...] = product_ref[pl.ds(at, rows), :]


def rotate_shares(me, pieces, basis, count):
    rows, width = sum(v.shape[0] for v in pieces), basis.shape[1]
    return call(
        functools.partial(rotate_shares_kernel, count),
        [((rows // count, width), jnp.float32)] * count,
        [SMEM] + [VMEM] * (len(pieces) + 1),
        me,
        *pieces,
        basis,
        scratch=[pltpu.VMEM((rows, width), jnp.float32)],
    )


def add_halve_kernel(j, me_ref, left_ref, right_ref, kept_ref, sent_ref):
    rows = kept_ref.shape[0]
    side = (me_ref[0] >> j) & 1
    for out_ref, at in ((kept_ref, side), (sent_ref, 1 - side)):
        span = pl.ds(pl.multiple_of(at * rows, rows), rows)
        out_ref[...] = left_ref[span, :] + right_ref[span, :]


def add_halve(me, pair, j):
    rows, width = pair[0].shape
    shape = ((rows // 2, width), jnp.float32)
    return call(functools.partial(add_halve_kernel, j), [shape] * 2, [SMEM, VMEM, VMEM], me, *pair)


def own_grads_kernel(me_ref, *refs):
    *feature_refs, basis_ref, out_ref, total_ref = refs
    d, k = pl.program_id(0), pl.program_id(1)
    block = basis_ref.shape[0]

    @pl.when(jnp.logical_and(d == 0, k == 0))
    def _():
        total_ref[...] = jnp.zeros_like(total_ref)

    for i, feature_ref in enumerate(feature_refs):

        @pl.when(d == i)
        def _(feature_ref=feature_ref):
            left = feature_ref[:, pl.ds(pl.multiple_of(k * block, block), block)]
            total_ref[...] += jnp.dot(left, basis_ref[...], preferred_element_type=jnp.float32)

    out_ref[...] = total_ref[...].astype(out_ref.dtype)


def own_grads(me, features, basis):
    rows, depth = features[0].shape
    width = basis.shape[1]
    block = next(n for n in (512, 256, 128, depth) if depth % n == 0)
    steps = depth // block
    return pl.pallas_call(
        own_grads_kernel,
        out_shape=jax.ShapeDtypeStruct((rows, width), jnp.bfloat16),
        grid_spec=pltpu.PrefetchScalarGridSpec(
            num_scalar_prefetch=1,
            grid=(len(features), steps),
            in_specs=[pl.BlockSpec((rows, depth), lambda d, k, me: (0, 0)) for _ in features]
            + [pl.BlockSpec((block, width), lambda d, k, me: ((me[0] ^ d) * steps + k, 0))],
            out_specs=pl.BlockSpec((rows, width), lambda d, k, me: (0, 0)),
            scratch_shapes=[pltpu.VMEM((rows, width), jnp.float32)],
        ),
        compiler_params=pltpu.CompilerParams(vmem_limit_bytes=SMALL_VMEM),
        cost_estimate=FREE,
    )(me, *features, basis)


def document_kernel(window, places, lengths_ref, me_ref, *refs):
    count = len(places)
    block_refs, (out_ref, rotated_ref, grads_ref, turned_ref, sems) = refs[:count], refs[count:]
    tokens, columns = grads_ref.shape
    documents = lengths_ref.shape[0]

    copies = []
    for n, (ref, (is_grads, row, rows, begin)) in enumerate(zip(block_refs, places)):
        source = ref.at[pl.ds(row, rows), :]
        if is_grads and ref.shape[1] > columns:
            source = ref.at[pl.ds(row, rows), pl.ds(ref.shape[1] - columns, columns)]
        at = pl.multiple_of(begin(me_ref[0], me_ref[1]), TILE)
        target = (grads_ref if is_grads else rotated_ref).at[pl.ds(at, rows), :]
        copies.append(pltpu.make_async_copy(source, target, sems.at[n]))
    for copy in copies:
        copy.start()
    for copy in copies:
        copy.wait()

    for at in range(0, tokens, window):
        turned_ref[:, at : at + window] = rotated_ref[at : at + window, :].T

    def product(block, first, last):
        base = pl.multiple_of(block * window, window)
        row = base + lax.broadcasted_iota(jnp.int32, (window, 1), 0)
        keep = jnp.logical_and(row >= first, row < last)
        right = grads_ref[pl.ds(base, window), :]
        right = jnp.where(keep, right, jnp.zeros_like(right))
        left = turned_ref[:, pl.ds(base, window)]
        return jnp.dot(left, right, preferred_element_type=jnp.float32)

    def add(s, value):
        value = value * value
        if s > 0:
            value = out_ref[...] + value
        if s == documents - 1:
            value = value * jnp.float32(1.0 / tokens)
        out_ref[...] = value

    first = jnp.int32(0)
    for s in range(documents):
        last = first + lengths_ref[s]
        low, high = first // window, (last - 1) // window

        @pl.when(low == high)
        def _(s=s, low=low, first=first, last=last):
            add(s, product(low, first, last))

        @pl.when(low != high)
        def _(s=s, low=low, high=high, first=first, last=last):
            add(s, product(low, first, last) + product(high, first, last))

        first = last


def document_squares(me, blocks, places, doc_lengths, tokens, width, columns):
    return pl.pallas_call(
        functools.partial(document_kernel, MAXLEN, places),
        out_shape=jax.ShapeDtypeStruct((width, columns), jnp.float32),
        in_specs=[SMEM, SMEM] + [ANY] * len(blocks),
        out_specs=VMEM,
        scratch_shapes=[
            pltpu.VMEM((tokens, width), jnp.bfloat16),
            pltpu.VMEM((tokens, columns), jnp.bfloat16),
            pltpu.VMEM((width, tokens), jnp.bfloat16),
            pltpu.SemaphoreType.DMA((len(blocks),)),
        ],
        compiler_params=pltpu.CompilerParams(vmem_limit_bytes=DOCUMENT_VMEM),
        cost_estimate=FREE,
    )(doc_lengths.astype(jnp.int32), me, *blocks)


def solution(mesh):
    n_dp, n_tensor = mesh.shape["dp"], mesh.shape["tensor"]
    order = ring_order(n_dp)
    forward = [(order[i], order[(i + 1) % n_dp]) for i in range(n_dp)]
    backward = [(d, s) for s, d in forward]
    swaps = {d: [(t, t ^ d) for t in range(n_tensor)] for d in range(1, n_tensor)}
    depth = n_tensor.bit_length() - 1

    def local(activations, in_basis, out_grads, out_basis, doc_lengths):
        shard = activations.shape[0]
        half = shard // 2
        tokens = shard * n_dp
        width, columns = in_basis.shape[1], out_basis.shape[1]
        basis = pltpu.with_memory_space_constraint(in_basis, pltpu.VMEM)

        mine = lax.axis_index("dp")
        spot = jnp.where(mine % 2 == 0, mine // 2, n_dp - 1 - mine // 2)
        me = jnp.stack([lax.axis_index("tensor"), spot]).astype(jnp.int32)
        activations, me = lax.optimization_barrier((activations, me))

        def begin_of(hops, row, owner_row):
            def begin(index, spot):
                at = row + owner_row(index)
                hop = hops[0] + at // shard if len(hops) > 1 else hops[0]
                way = (at % shard) // half
                place = lax.rem(spot + jnp.where(way == 0, n_dp - hop, hop), jnp.int32(n_dp))
                source = jnp.where(2 * place < n_dp, 2 * place, 2 * (n_dp - 1 - place) + 1)
                return source * shard + at % shard

            return begin

        def halves(block):
            return [block[:half], block[half:]]

        def pass_on(pieces):
            return [lax.ppermute(v, "dp", p) for v, p in zip(pieces, (forward, backward))]

        def swap(block, d):
            return lax.ppermute(block, "tensor", swaps[d])

        stages = [("halve", j) for j in range(1, depth)]
        stages += [("collect", j) for j in reversed(range(depth))]

        def stage(k, state):
            kind, j = stages[k]
            held, came = state
            if kind == "halve":
                kept, sent = add_halve(me, (held, came), j)
                return kept, swap(sent, 1 << j)
            if j == depth - 1:
                held = (held + came).astype(jnp.bfloat16)
            else:
                held = jnp.concatenate([held, came], 0)
            return held, swap(held, 1 << j)

        def direct_middle(parts):
            total = functools.reduce(jnp.add, parts).astype(jnp.bfloat16)
            return [total] + [swap(total, d) for d in range(1, n_tensor)]

        hops = n_dp - 1 + LAG
        groups = [[h, h + 1] for h in range(0, n_dp, 2)]
        if shard // n_tensor >= TILE:
            groups = groups[:-1] + [[n_dp - 2], [n_dp - 1]]

        act = {0: halves(activations)}
        grads, sums = {}, {}
        flight = pass_on(act[0])
        features = [out_grads] + [swap(out_grads, d) for d in range(1, n_tensor)]
        due = {2: [("features", 0, features)]}

        def later(hop, kind, i, value):
            due.setdefault(hop, []).append((kind, i, value))

        def start_shares(group):
            parts = rotate_shares(me, [v for h in group for v in act[h]], basis, n_tensor)
            return [parts[0]] + [swap(parts[d], d) for d in range(1, n_tensor)]

        for hop in range(1, hops + 1):
            ready = due.pop(hop, [])
            bundle = (flight, [value for _, _, value in ready])
            arrived, values = lax.optimization_barrier(bundle)
            got = {(kind, i): value for (kind, i, _), value in zip(ready, values)}
            if ("features", 0) in got:
                later(hop + 1, "own", 0, own_grads(me, got["features", 0], out_basis))
            if ("own", 0) in got:
                grads[0] = halves(got["own", 0])
            if hop < n_dp:
                act[hop] = arrived
            if hop > LAG:
                grads[hop - LAG] = arrived
            moving = arrived
            if hop == LAG:
                moving = [jnp.concatenate([v, g], 1) for v, g in zip(arrived, grads[0])]
            if hop == n_dp - 1:
                moving = [v[:, -columns:] for v in arrived]
            if hop < hops:
                flight = pass_on(moving)
            for (kind, i), value in got.items():
                if kind == "product":
                    later(hop + 1, 0, i, (value[0], swap(value[1], 1)))
                elif kind == "shares":
                    later(hop + 1, "total", i, direct_middle(value))
                elif kind == "total" or kind == len(stages):
                    sums[i] = value
                elif isinstance(kind, int):
                    later(hop + 1, kind + 1, i, stage(kind, value))
            for i, group in enumerate(groups):
                if group[-1] != hop:
                    continue
                if len(group) == 1 and hop == n_dp - 1:
                    sums[i] = direct_middle(start_shares(group))
                elif len(group) == 1:
                    later(hop + 1, "shares", i, start_shares(group))
                else:
                    product = rotate_pair(me, [v for h in group for v in act[h]], basis)
                    if hop < n_dp - 3:
                        later(hop + 1, "product", i, product)
                    else:
                        later(hop + 1, 0, i, (product[0], swap(product[1], 1)))

        for _, items in sorted(due.items()):
            for kind, i, value in items:
                if isinstance(kind, int):
                    for k in range(kind, len(stages)):
                        value = stage(k, value)
                sums[i] = value

        blocks, places = [], []
        for i, group in enumerate(groups):
            if len(group) == 1:
                rows = shard // n_tensor
                for d, block in enumerate(sums[i]):
                    owner_row = lambda me, d=d, rows=rows: (me ^ d) * rows
                    blocks.append(block)
                    places.append((False, 0, rows, begin_of(group, 0, owner_row)))
                continue
            rows = 2 * shard // n_tensor
            around = [0]
            for j in reversed(range(depth)):
                around = around + [d ^ (1 << j) for d in around]
            for n, d in enumerate(around):

                def owner_row(me, d=d):
                    bits = [((me ^ d) >> j) & 1 for j in range(depth)]
                    return sum(bit * (2 * shard >> (j + 1)) for j, bit in enumerate(bits))

                block = sums[i][2 * n // len(around)]
                blocks.append(block)
                row = n % (len(around) // 2) * rows
                places.append((False, row, rows, begin_of(group, 0, owner_row)))
        for h, pieces in grads.items():
            for way, piece in enumerate(pieces):
                blocks.append(piece)
                owner_row = lambda me, way=way: jnp.int32(way * half)
                places.append((True, 0, half, begin_of([h], 0, owner_row)))
        return document_squares(me, blocks, places, doc_lengths, tokens, width, columns)

    placed = (P("dp", "tensor"), P("tensor", "dp"), P("dp", "tensor"), P(None, "tensor"), P())
    return jax.shard_map(
        local, mesh=mesh, in_specs=placed, out_specs=P("dp", "tensor"), check_vma=False
    )
```

```python
import functools

import jax
import jax.numpy as jnp
from jax import lax
from jax.experimental import pallas as pl
from jax.experimental.pallas import tpu as pltpu
from jax.sharding import PartitionSpec as P

MAXLEN = 256
GRAIN = 128
TILE = 16
SMALL_VMEM = 8 * 1024 * 1024
DOCUMENT_VMEM = 32 * 1024 * 1024
FREE = pl.CostEstimate(flops=0, bytes_accessed=0, transcendentals=0)
SMEM = pl.BlockSpec(memory_space=pltpu.SMEM)
VMEM = pl.BlockSpec(memory_space=pltpu.VMEM)


def ring_order(count):
    return list(range(0, count, 2)) + list(range(1, count, 2))[::-1]


def call(kernel, shapes, in_specs, *operands, scratch=()):
    return pl.pallas_call(
        kernel,
        out_shape=[jax.ShapeDtypeStruct(*shape) for shape in shapes],
        in_specs=in_specs,
        out_specs=[VMEM] * len(shapes),
        scratch_shapes=list(scratch),
        compiler_params=pltpu.CompilerParams(vmem_limit_bytes=SMALL_VMEM),
        cost_estimate=FREE,
    )(*operands)


def product_of(piece_refs, basis_ref):
    pieces = [ref[...] for ref in piece_refs]
    return jnp.dot(
        jnp.concatenate(pieces, 0), basis_ref[...], preferred_element_type=jnp.float32
    )


def rotate_shares_kernel(count, me_ref, *refs):
    piece_refs, (basis_ref, *share_refs, product_ref) = refs[:-count - 2], refs[-count - 2 :]
    product_ref[...] = product_of(piece_refs, basis_ref)
    rows = share_refs[0].shape[0]
    for d, share_ref in enumerate(share_refs):
        at = pl.multiple_of((me_ref[0] ^ d) * rows, rows)
        share_ref[...] = product_ref[pl.ds(at, rows), :]


def rotate_shares(me, pieces, basis, count):
    rows, width = sum(v.shape[0] for v in pieces), basis.shape[1]
    return call(
        functools.partial(rotate_shares_kernel, count),
        [((rows // count, width), jnp.float32)] * count,
        [SMEM] + [VMEM] * (len(pieces) + 1),
        me,
        *pieces,
        basis,
        scratch=[pltpu.VMEM((rows, width), jnp.float32)],
    )


def own_grads_kernel(me_ref, *refs):
    *feature_refs, basis_ref, out_ref, total_ref = refs
    d, k = pl.program_id(0), pl.program_id(1)
    block = basis_ref.shape[0]

    @pl.when(jnp.logical_and(d == 0, k == 0))
    def _():
        total_ref[...] = jnp.zeros_like(total_ref)

    for i, feature_ref in enumerate(feature_refs):

        @pl.when(d == i)
        def _(feature_ref=feature_ref):
            left = feature_ref[:, pl.ds(pl.multiple_of(k * block, block), block)]
            total_ref[...] += jnp.dot(left, basis_ref[...], preferred_element_type=jnp.float32)

    out_ref[...] = total_ref[...].astype(out_ref.dtype)


def own_grads(me, features, basis):
    rows, depth = features[0].shape
    width = basis.shape[1]
    block = next(n for n in (1024, 512, 256, 128, depth) if depth % n == 0)
    steps = depth // block
    return pl.pallas_call(
        own_grads_kernel,
        out_shape=jax.ShapeDtypeStruct((rows, width), jnp.bfloat16),
        grid_spec=pltpu.PrefetchScalarGridSpec(
            num_scalar_prefetch=1,
            grid=(len(features), steps),
            in_specs=[pl.BlockSpec((rows, depth), lambda d, k, me: (0, 0)) for _ in features]
            + [pl.BlockSpec((block, width), lambda d, k, me: ((me[0] ^ d) * steps + k, 0))],
            out_specs=pl.BlockSpec((rows, width), lambda d, k, me: (0, 0)),
            scratch_shapes=[pltpu.VMEM((rows, width), jnp.float32)],
        ),
        compiler_params=pltpu.CompilerParams(vmem_limit_bytes=SMALL_VMEM),
        cost_estimate=FREE,
    )(me, *features, basis)


def document_kernel(window, places, lengths_ref, me_ref, *refs):
    count = len(places)
    block_refs, (out_ref, *scratch) = refs[:count], refs[count:]
    rotated_ref, grads_ref, turned_ref, total_ref, out_sems = scratch
    tokens, columns = grads_ref.shape
    documents = lengths_ref.shape[0]

    for ref, (is_grads, row, rows, begin) in zip(block_refs, places):
        at = pl.multiple_of(begin(me_ref[0], me_ref[1]), TILE)
        target = grads_ref if is_grads else rotated_ref
        target[pl.ds(at, rows), :] = ref[row : row + rows, :]
    for at in range(0, tokens, window):
        turned_ref[:, at : at + window] = rotated_ref[at : at + window, :].T

    width = out_ref.shape[0]
    strip = min(width, 256)

    def add(s, size, first, last):
        base = jnp.minimum(first // GRAIN * GRAIN, tokens - size)
        base = pl.multiple_of(base, GRAIN)
        row = base + lax.broadcasted_iota(jnp.int32, (size, 1), 0)
        keep = jnp.logical_and(row >= first, row < last)
        right = grads_ref[pl.ds(base, size), :]
        right = jnp.where(keep, right, jnp.zeros_like(right))
        ends = s == documents - 1
        for at in range(0, width, strip if ends else width):
            span = slice(at, at + strip if ends else width)
            left = turned_ref[span, pl.ds(base, size)]
            value = jnp.dot(left, right, preferred_element_type=jnp.float32)
            value = value * value
            if s > 0:
                value = total_ref[span, :] + value
            if ends:
                value = value * jnp.float32(1.0 / tokens)
            total_ref[span, :] = value
            if ends:
                out_copy(at).start()

    def out_copy(at):
        span = pl.ds(at, strip)
        return pltpu.make_async_copy(
            total_ref.at[span, :], out_ref.at[span, :], out_sems.at[at // strip]
        )

    first = jnp.int32(0)
    for s in range(documents):
        last = first + lengths_ref[s]
        fits = last <= jnp.minimum(first // GRAIN * GRAIN, tokens - window) + window
        pl.when(fits)(functools.partial(add, s, window, first, last))
        pl.when(jnp.logical_not(fits))(functools.partial(add, s, window + GRAIN, first, last))
        first = last
    for at in range(0, width, strip):
        out_copy(at).wait()


def document_squares(me, blocks, places, doc_lengths, tokens, width, columns):
    return pl.pallas_call(
        functools.partial(document_kernel, MAXLEN, places),
        out_shape=jax.ShapeDtypeStruct((width, columns), jnp.float32),
        in_specs=[SMEM, SMEM] + [VMEM] * len(blocks),
        out_specs=pl.BlockSpec(memory_space=pltpu.HBM),
        scratch_shapes=[
            pltpu.VMEM((tokens, width), jnp.bfloat16),
            pltpu.VMEM((tokens, columns), jnp.bfloat16),
            pltpu.VMEM((width, tokens), jnp.bfloat16),
            pltpu.VMEM((width, columns), jnp.float32),
            pltpu.SemaphoreType.DMA((max(1, width // 256),)),
        ],
        compiler_params=pltpu.CompilerParams(vmem_limit_bytes=DOCUMENT_VMEM),
        cost_estimate=FREE,
    )(doc_lengths.astype(jnp.int32), me, *blocks)


def solution(mesh):
    n_dp, n_tensor = mesh.shape["dp"], mesh.shape["tensor"]
    order = ring_order(n_dp)
    forward = [(order[i], order[(i + 1) % n_dp]) for i in range(n_dp)]
    backward = [(d, s) for s, d in forward]
    swaps = {d: [(t, t ^ d) for t in range(n_tensor)] for d in range(1, n_tensor)}
    last = n_dp // 2

    def local(activations, in_basis, out_grads, out_basis, doc_lengths):
        shard = activations.shape[0]
        half = shard // 2
        tokens = shard * n_dp
        width, columns = in_basis.shape[1], out_basis.shape[1]
        basis = pltpu.with_memory_space_constraint(in_basis, pltpu.VMEM)
        out_basis = pltpu.with_memory_space_constraint(out_basis, pltpu.HBM)

        mine = lax.axis_index("dp")
        spot = jnp.where(mine % 2 == 0, mine // 2, n_dp - 1 - mine // 2)
        me = jnp.stack([lax.axis_index("tensor"), spot]).astype(jnp.int32)
        activations, me = lax.optimization_barrier((activations, me))

        def start_of(hop, way):
            def start(spot):
                place = lax.rem(spot + (n_dp - hop if way == 0 else hop), jnp.int32(n_dp))
                source = jnp.where(2 * place < n_dp, 2 * place, 2 * (n_dp - 1 - place) + 1)
                return source * shard + (half if hop == last and way == 1 else 0)

            return start

        def share_of(pieces, d, rows):
            def begin(index, spot):
                at, low = (index ^ d) * rows, 0
                token = jnp.int32(0)
                for start, size in pieces:
                    inside = jnp.logical_and(at >= low, at < low + size)
                    token = jnp.where(inside, start(spot) + at - low, token)
                    low += size
                return token

            return begin

        def pass_on(hop, pieces):
            if hop == last:
                pieces = [pieces[0][:half], pieces[1][half:]]
            return [lax.ppermute(v, "dp", p) for v, p in zip(pieces, (forward, backward))]

        def swap(block, d):
            return lax.ppermute(block, "tensor", swaps[d])

        def send_shares(parts):
            return [parts[0]] + [swap(parts[d], d) for d in range(1, n_tensor)]

        def send_total(parts):
            total = functools.reduce(jnp.add, parts).astype(jnp.bfloat16)
            return [total] + [swap(total, d) for d in range(1, n_tensor)]

        groups = {hop: [hop] for hop in range(last + 1)}
        if shard // n_tensor < TILE:
            groups[last] = groups.pop(0) + groups[last]

        act, grads, sums = {0: [activations]}, {}, {}
        flight = {("act", 1): pass_on(1, [activations] * 2)}
        features = [out_grads] + [swap(out_grads, d) for d in range(1, n_tensor)]
        flight["grads", 0] = [own_grads(me, features, out_basis)]

        def rotate(group):
            return rotate_shares(me, [v for h in group for v in act[h]], basis, n_tensor)

        if 0 in groups:
            flight["shares", 0] = send_shares(rotate(groups[0]))
        def settle(flight):
            keys = list(flight)
            return dict(zip(keys, lax.optimization_barrier([flight[key] for key in keys])))

        for hop in range(1, last + 2):
            behind = {}
            if 1 < hop <= last:
                early = {key: flight.pop(key) for key in list(flight) if key[0] != "sums"}
                later = {key: early.pop(key) for key in [("act", hop)]}
                early = settle(early)
                grads[hop - 1] = early.pop(("grads", hop - 1))
                for (_, i), value in early.items():
                    total = send_total(value)
                    (behind if hop == last else flight)["sums", i] = total
                flight.update(later)
            came, flight = settle(flight), behind
            for (kind, i), value in came.items():
                if kind == "shares":
                    flight["sums", i] = send_total(value)
                else:
                    {"act": act, "grads": grads, "sums": sums}[kind][i] = value
            if hop < last:
                flight["act", hop + 1] = pass_on(hop + 1, act[hop])
            if hop <= last:
                shares = rotate(groups[hop])
                gradients = grads[hop - 1]
                if hop == last:
                    shares, gradients = lax.optimization_barrier((list(shares), gradients))
                flight["grads", hop] = pass_on(hop, gradients * (2 if hop == 1 else 1))
                flight["shares", hop] = send_shares(shares)
        for (_, i), value in flight.items():
            sums[i] = value

        blocks, places = [], []
        for i, group in groups.items():
            pieces = [(start_of(h, way), v.shape[0]) for h in group for way, v in enumerate(act[h])]
            rows = sum(size for _, size in pieces) // n_tensor
            for d, block in enumerate(sums[i]):
                blocks.append(block)
                places.append((False, 0, rows, share_of(pieces, d, rows)))
        for h, pieces in grads.items():
            for way, piece in enumerate(pieces):
                start = start_of(h, way)
                blocks.append(piece)
                places.append((True, 0, piece.shape[0], lambda me, spot, start=start: start(spot)))
        return document_squares(me, blocks, places, doc_lengths, tokens, width, columns)

    placed = (P("dp", "tensor"), P("tensor", "dp"), P("dp", "tensor"), P(None, "tensor"), P())
    return jax.shard_map(
        local, mesh=mesh, in_specs=placed, out_specs=P("dp", "tensor"), check_vma=False
    )
```
